256 devices in a mesh: replica: 4 (over y_hi, core), fsdp: 64 (over x, y_lo, z).
Axes of the slice: x: 4, y: 4 (y_hi: 2, y_lo: 2; y = y_hi * 2 + y_lo), z: 8, core: 2. Of those that a mesh axis runs over, the one named last changes fastest.
Arguments:
- tokens_in: bfloat16 [4, 24576, 8192], P('replica', 'fsdp'), may hold values from -16 to 16
- targets: bfloat16 [4, 24576, 512], P('replica', 'fsdp'), may hold values from -6 to 6
- weights: float32 [4, 8192, 512], P('replica', 'fsdp'), may hold values from -6 to 6
- adam_mean: float32 [4, 8192, 512], P('replica', 'fsdp'), may hold values from -6 to 6
- adam_var: float32 [4, 8192, 512], P('replica', 'fsdp'), may hold values from 0.5 to 8
- anchor: float32 [8192, 512], P('fsdp'), may hold values from -6 to 6
- outer_momentum: float32 [8192, 512], P('fsdp'), may hold values from -6 to 6
- pseudo_grad: float32 [4, 8192, 128], P('replica', 'fsdp'), may hold values from -6 to 6
- fragment: int32 [], replicated, may hold values from 0 to 3
- delay: int32 [4], P('replica'), may hold values from 0 to 1, as said below
Outputs:
- new_weights: float32 [4, 8192, 512], P('replica', 'fsdp')
- new_adam_mean: float32 [4, 8192, 512], P('replica', 'fsdp')
- new_adam_var: float32 [4, 8192, 512], P('replica', 'fsdp')
- new_anchor: float32 [8192, 512], P('fsdp')
- new_momentum: float32 [8192, 512], P('fsdp')
The draws below stay inside these ranges and needn't reach their ends.
Inputs may be any that keep to these rules, and one draw needn't show every extreme that they name: Exactly 2 of the workers have delay 1, the others 0.
All inputs are finite; a program needn't handle non-finite values.
Results may differ from the reference program's by a relative error of at most 0.00053.
Values may be sent and summed in bfloat16 or wider, within the bound.
No kernel may reach another device: no remote copies, remote signals or barrier semaphores. Data moves between devices by JAX's collectives and lax.ppermute only.
A program may use at most 128 MiB of HBM per device.

```python
import math
import jax
import jax.numpy as jnp
from jax import lax

D = 8192
KW = 512
HEAD = 128
TOKENS = 24576
WORKERS = 4
N_REPLICA = 4


def draw_delay(key, part):
    key = jax.random.fold_in(key, 5)
    order = jax.random.permutation(key, WORKERS)
    return (order < WORKERS // 2).astype(jnp.int32)


def strengthened(values, stream_key, source, target, blocks, factor):
    owner, partner = [(jnp.arange(values.shape[dim]) // (values.shape[dim] // blocks)).reshape([-1 if axis == dim else 1 for axis in range(values.ndim)]) for dim in (source, target)]
    chosen = jax.random.permutation(stream_key, blocks)[partner]
    strong = (owner == chosen) | (owner == (partner + blocks // 2) % blocks)
    return jnp.where(strong, factor * values, values)


def shard_levels(own_key, extent, pieces, smallest, largest):
    def one(position, shards_of):
        steps = jax.random.uniform(jax.random.fold_in(jax.random.fold_in(own_key, 6), position), (shards_of,), jnp.float32, smallest / len(pieces), largest / len(pieces))
        return jnp.repeat(jnp.exp(steps), extent[position] // shards_of).reshape((-1,) + (1,) * (len(extent) - position - 1))

    loudness = one(*pieces[0])
    for cut in pieces[1:]:
        loudness = loudness * one(*cut)
    return loudness


def normal_values(rng, extent, scale, limit, split=(), dtype=jnp.bfloat16):
    gain = shard_levels(rng, extent, split, -0.22, 0.18) if split else 1.0
    drawn = jax.random.normal(rng, extent, jnp.float32) * scale * gain
    return jnp.minimum(jnp.maximum(drawn, -limit), limit).astype(dtype)


def heavy_noise(stream_key, shape, spread, reach, split, heavy, held_as=jnp.bfloat16):
    values = spread * jax.random.normal(stream_key, shape, jnp.float32)
    if split:
        values = values * shard_levels(stream_key, shape, split, -0.22, 0.18)
    return jnp.clip(strengthened(values, jax.random.fold_in(stream_key, 3), *heavy), -reach, reach).astype(held_as)


def setup_inputs(seed: int = 0) -> dict:
    streams_of = jax.random.split(jax.random.key(seed), 11)
    tokens_in = heavy_noise(streams_of[0], (WORKERS, TOKENS, D), 1.0, 16.0, ((0, 4), (1, 64)), (1, 2, 64, 4.0))
    targets = normal_values(streams_of[1], (WORKERS, TOKENS, KW), 1.0, 6.0, ((0, 4), (1, 64)))
    weights = normal_values(streams_of[2], (WORKERS, D, KW), 1.0, 6.0, ((0, 4), (1, 64)), jnp.float32)
    adam_mean = normal_values(streams_of[3], (WORKERS, D, KW), 1.5, 6.0, ((0, 4), (1, 64)), jnp.float32)
    adam_var = jnp.clip(jnp.exp(math.log(8.0) - 2.7725887 * jax.random.uniform(streams_of[4], (WORKERS, D, KW), jnp.float32) ** shard_levels(streams_of[4], (WORKERS, D, KW), ((0, 4), (1, 64)), -0.2, 0.2)), 0.5, 8.0)
    anchor = normal_values(streams_of[5], (D, KW), 1.0, 6.0, ((0, 64),), jnp.float32)
    outer_momentum = normal_values(streams_of[6], (D, KW), 0.5, 6.0, ((0, 64),), jnp.float32)
    pseudo_grad = normal_values(streams_of[7], (WORKERS, D, HEAD), 0.5, 6.0, ((0, 4), (1, 64)), jnp.float32)
    fragment = jax.random.randint(streams_of[8], (), 0, KW // HEAD).astype(jnp.int32)
    delay = draw_delay(jax.random.fold_in(streams_of[10], 71), 0)
    return {"tokens_in": tokens_in, "targets": targets, "weights": weights, "adam_mean": adam_mean, "adam_var": adam_var, "anchor": anchor, "outer_momentum": outer_momentum, "pseudo_grad": pseudo_grad, "fragment": fragment, "delay": delay}


beta_first = 0.9
beta_second = 0.95
adam_epsilon = 1e-08
adam_steps = 20.0
inner_rate = 0.1
weight_decay = 0.1
outer_rate = 0.7
outer_pull = 0.9
blend_share = 0.5
norm_epsilon = 1e-05

def blend(field, anchor_next, offset):
    piece = lax.dynamic_slice_in_dim(field, offset, anchor_next.shape[1], 1)
    mixed = blend_share * anchor_next + (1.0 - blend_share) * piece
    return lax.dynamic_update_slice_in_dim(field, mixed, offset, 1)

def normalize(rows):
    wide = rows.astype(jnp.float32)
    stat = lax.optimization_barrier(jnp.mean(wide * wide, axis=-1, keepdims=True))
    return (wide * lax.rsqrt(stat + norm_epsilon)).astype(jnp.bfloat16)

def adam_update(start_field, grad, first, second):
    mean_next = beta_first * first + (1.0 - beta_first) * grad
    var_next = beta_second * second + (1.0 - beta_second) * grad * grad
    first_fix = 1.0 - beta_first ** adam_steps
    second_fix = 1.0 - beta_second ** adam_steps
    ratio = mean_next / first_fix / (jnp.sqrt(var_next / second_fix) + adam_epsilon)
    return (start_field - inner_rate * (ratio + weight_decay * start_field), mean_next, var_next)

def reference(tokens_in, targets, weights, adam_mean, adam_var, anchor, outer_momentum, pseudo_grad, fragment, delay):
    average = lax.optimization_barrier(jnp.sum(pseudo_grad, axis=0)) / N_REPLICA
    offset = (fragment * HEAD).astype(jnp.int32)
    anchor_piece = lax.dynamic_slice_in_dim(anchor, offset, HEAD, 1)
    moment_piece = lax.dynamic_slice_in_dim(outer_momentum, offset, HEAD, 1)
    moment_next = outer_pull * moment_piece + average
    anchor_next = anchor_piece - outer_rate * (average + outer_pull * moment_next)
    new_anchor = lax.dynamic_update_slice_in_dim(anchor, anchor_next, offset, 1)
    new_momentum = lax.dynamic_update_slice_in_dim(outer_momentum, moment_next, offset, 1)
    key_scale = 1.0 / math.sqrt(D)
    grad_scale = 1.0 / math.sqrt(TOKENS)
    results = []
    means = []
    variances = []
    for worker in range(N_REPLICA):
        local = weights[worker]
        flag = delay[worker]
        start_field = jnp.where(flag == 0, blend(local, anchor_next, offset), local)
        normed = normalize(tokens_in[worker])
        keys = jnp.dot(normed, start_field.astype(jnp.bfloat16), preferred_element_type=jnp.float32)
        residual = (keys * key_scale - targets[worker].astype(jnp.float32)).astype(jnp.bfloat16)
        grad = lax.dot_general(normed, residual, (((0,), (0,)), ((), ())), preferred_element_type=jnp.float32) * grad_scale
        stepped, mean_next, var_next = adam_update(start_field, grad, adam_mean[worker], adam_var[worker])
        results.append(jnp.where(flag == 1, blend(stepped, anchor_next, offset), stepped))
        means.append(mean_next)
        variances.append(var_next)
    return (jnp.stack(results), jnp.stack(means), jnp.stack(variances), new_anchor, new_momentum)
```

```python
import math

import jax
import jax.numpy as jnp
from jax import lax
from jax.sharding import PartitionSpec as P

beta_first = 0.9
beta_second = 0.95
adam_epsilon = 1e-08
adam_steps = 20.0
inner_rate = 0.1
weight_decay = 0.1
outer_rate = 0.7
outer_pull = 0.9
blend_share = 0.5
norm_epsilon = 1e-05

NX, NY, NZ = 4, 2, 8
NXY = NX * NY
HEADS = 4


def fsdp_index(x, y, z):
    return (x % NX * NY + y % NY) * NZ + z % NZ


def shift(dx, dy, dz):
    return [
        (fsdp_index(x, y, z), fsdp_index(x + dx, y + dy, z + dz))
        for x in range(NX)
        for y in range(NY)
        for z in range(NZ)
    ]


X_UP, X_DOWN, Y_SWAP = shift(1, 0, 0), shift(-1, 0, 0), shift(0, 1, 0)
Z_UP, Z_DOWN = shift(0, 0, 1), shift(0, 0, -1)
Z_GROUPS = [[xy * NZ + z for z in range(NZ)] for xy in range(NXY)]
XY_GROUPS = [[xy * NZ + z for xy in range(NXY)] for z in range(NZ)]


def send(values, pairs):
    return lax.ppermute(values, "fsdp", pairs)


def exchange(values, groups):
    return lax.all_to_all(values, "fsdp", 0, 0, axis_index_groups=groups, tiled=True)


def normalize(rows):
    wide = rows.astype(jnp.float32)
    stat = jnp.mean(wide * wide, axis=-1, keepdims=True)
    return (wide * lax.rsqrt(stat + norm_epsilon)).astype(jnp.bfloat16)


def adam_update(start_field, grad, first, second):
    mean_next = beta_first * first + (1.0 - beta_first) * grad
    var_next = beta_second * second + (1.0 - beta_second) * grad * grad
    first_fix = 1.0 - beta_first**adam_steps
    second_fix = 1.0 - beta_second**adam_steps
    ratio = mean_next / first_fix / (jnp.sqrt(var_next / second_fix) + adam_epsilon)
    return (start_field - inner_rate * (ratio + weight_decay * start_field), mean_next, var_next)


def heads_of(field):
    size = field.shape[-1] // HEADS
    return [field[..., i * size : (i + 1) * size] for i in range(HEADS)]


def pick(choices, which):
    out = choices[0]
    for i in range(1, HEADS):
        out = jnp.where(which == i, choices[i], out)
    return out


def replace_head(field, piece, fragment):
    return jnp.concatenate(
        [jnp.where(fragment == i, piece, head) for i, head in enumerate(heads_of(field))], axis=-1
    )


def pack(total, terms):
    return (total * (0.5 / terms)).astype(jnp.float16)


def unpack(message, terms):
    return message.astype(jnp.float32) * (2.0 * terms)


def gather_a(shard, x, y):
    rows, cols = shard.shape
    own = exchange(jnp.broadcast_to(shard, (NZ, rows, cols)), Z_GROUPS).reshape(NZ * rows, cols)
    low = send(own, X_UP)
    high = send(own, X_DOWN)
    side = send(own, Y_SWAP)
    far = send(high, X_DOWN)
    low_side = send(side, X_UP)
    high_side = send(high, Y_SWAP)
    a, b = thirds(NZ * rows)
    far_side = (
        send(high_side[:a], X_DOWN),
        send(low_side[a:b], X_UP),
        send(far[b:], Y_SWAP),
    )
    whole = jnp.zeros((NXY, NZ * rows, cols), shard.dtype)
    for dx, dy, piece in (
        (0, 0, own),
        (-1, 0, low),
        (1, 0, high),
        (0, 1, side),
        (2, 0, far),
        (-1, 1, low_side),
        (1, 1, high_side),
    ):
        whole = lax.dynamic_update_slice(whole, piece[None], (block_of(x + dx, y + dy), 0, 0))
    for start, piece in zip((0, a, b), far_side):
        whole = lax.dynamic_update_slice(whole, piece[None], (block_of(x + 2, y + 1), start, 0))
    return whole.reshape(NXY * NZ * rows, cols)


def thirds(rows):
    step = rows // 3 // 16 * 16
    return step, 2 * step


def block_of(x, y):
    return (x + NX) % NX * NY + (y + NY) % NY


def gather_b(shard, z):
    rows, cols = shard.shape
    own = exchange(jnp.broadcast_to(shard, (NXY, rows, cols)), XY_GROUPS).reshape(NXY, rows, cols)
    whole = jnp.zeros((NXY, NZ, rows, cols), shard.dtype)
    whole = lax.dynamic_update_slice(whole, own[:, None], (0, z, 0, 0))
    up, down = own, own
    half = NXY // 2
    for step in range(1, NZ // 2):
        up, down = send(up, Z_UP), send(down, Z_DOWN)
        whole = lax.dynamic_update_slice(whole, up[:, None], (0, (z - step) % NZ, 0, 0))
        whole = lax.dynamic_update_slice(whole, down[:, None], (0, (z + step) % NZ, 0, 0))
    up, down = send(up[:half], Z_UP), send(down[half:], Z_DOWN)
    whole = lax.dynamic_update_slice(whole, up[:, None], (0, (z + NZ // 2) % NZ, 0, 0))
    whole = lax.dynamic_update_slice(whole, down[:, None], (half, (z + NZ // 2) % NZ, 0, 0))
    return whole.reshape(NXY * NZ * rows, cols)


def scatter_a(partial, x, y):
    rows, cols = partial.shape[0] // (NXY * NZ), partial.shape[1]
    blocks = partial.reshape(NXY, NZ * rows, cols)

    def mine(dx, dy, start=0, stop=NZ * rows):
        return lax.dynamic_slice(
            blocks, (block_of(x + dx, y + dy), start, 0), (1, stop - start, cols)
        )[0]

    a, b = thirds(NZ * rows)
    end = NZ * rows
    to_high_side = unpack(send(pack(mine(2, 1, 0, a), 1), X_UP), 1)
    to_low_side = unpack(send(pack(mine(2, 1, a, b), 1), X_DOWN), 1)
    to_far = unpack(send(pack(mine(2, 1, b, end), 1), Y_SWAP), 1)
    far = jnp.concatenate([mine(2, 0, 0, b), mine(2, 0, b, end) + to_far])
    low_side = jnp.concatenate(
        [mine(-1, 1, 0, a), mine(-1, 1, a, b) + to_low_side, mine(-1, 1, b, end)]
    )
    high_side = jnp.concatenate([mine(1, 1, 0, a) + to_high_side, mine(1, 1, a, end)])
    from_far = unpack(send(pack(far, 2), X_UP), 2)
    from_low_side = unpack(send(pack(low_side, 2), X_DOWN), 2)
    from_high_side = unpack(send(pack(high_side, 2), Y_SWAP), 2)
    high = unpack(send(pack(mine(1, 0) + from_far + from_high_side, 8), X_UP), 8)
    low = unpack(send(pack(mine(-1, 0), 8), X_DOWN), 8)
    side = unpack(send(pack(mine(0, 1) + from_low_side, 8), Y_SWAP), 8)
    total = mine(0, 0) + high + low + side
    message = pack(total, 8).reshape(NZ, rows, cols)
    return jnp.sum(unpack(exchange(message, Z_GROUPS).reshape(NZ, rows, cols), 8), axis=0)


def scatter_b(partial, z):
    rows, cols = partial.shape[0] // (NXY * NZ), partial.shape[1]
    blocks = partial.reshape(NXY, NZ, rows, cols)
    half = NXY // 2

    def mine(dz, start=0, stop=NXY):
        return lax.dynamic_slice(
            blocks, (start, (z + dz + NZ) % NZ, 0, 0), (stop - start, 1, rows, cols)
        )[:, 0]

    up = unpack(send(pack(mine(4, 0, half), 4), Z_UP), 4)
    down = unpack(send(pack(mine(-4, half, NXY), 4), Z_DOWN), 4)
    up = jnp.concatenate([mine(3, 0, half) + up, mine(3, half, NXY)])
    down = jnp.concatenate([mine(-3, 0, half), mine(-3, half, NXY) + down])
    for step in (2, 1, 0):
        up = unpack(send(pack(up, 4), Z_UP), 4)
        down = unpack(send(pack(down, 4), Z_DOWN), 4)
        if step:
            up, down = mine(step) + up, mine(-step) + down
    total = mine(0) + up + down
    return jnp.sum(
        unpack(exchange(pack(total, 8), XY_GROUPS).reshape(NXY, rows, cols), 8), axis=0
    )


def on_device(
    tokens_in,
    targets,
    weights,
    adam_mean,
    adam_var,
    anchor,
    outer_momentum,
    pseudo_grad,
    fragment,
    delay,
):
    width = tokens_in.shape[2]
    total_tokens = tokens_in.shape[1] * lax.axis_size("fsdp")
    flag = delay[0]
    position = lax.axis_index("fsdp")
    x, y, z = position // (NY * NZ), position // NZ % NY, position % NZ

    with jax.named_scope("outer_update"):
        summed = pseudo_grad[0]
        summed = summed + lax.ppermute(summed, "replica", [(0, 1), (1, 0), (2, 3), (3, 2)])
        summed = summed + lax.ppermute(summed, "replica", [(0, 2), (2, 0), (1, 3), (3, 1)])
        average = summed / lax.axis_size("replica")
        moment_next = outer_pull * pick(heads_of(outer_momentum), fragment) + average
        anchor_next = pick(heads_of(anchor), fragment) - outer_rate * (
            average + outer_pull * moment_next
        )
        new_anchor = replace_head(anchor, anchor_next, fragment)
        new_momentum = replace_head(outer_momentum, moment_next, fragment)

    local = weights[0]
    local_heads = heads_of(local)
    local_piece = pick(local_heads, fragment)
    merged = blend_share * anchor_next + (1.0 - blend_share) * local_piece
    start_piece = jnp.where(flag == 0, merged, local_piece)
    start_field = replace_head(local, start_piece, fragment)

    def rolled(heads, k):
        return pick(heads, (fragment + 1 + k) % HEADS)

    shard_a = jnp.concatenate([rolled(local_heads, 0), rolled(local_heads, 1)], axis=1)
    shard_b = jnp.concatenate([rolled(local_heads, 2), start_piece], axis=1)
    with jax.named_scope("gather_b"):
        field_b = gather_b(shard_b.astype(jnp.bfloat16), z)
    with jax.named_scope("gather_a"):
        field_a = gather_a(shard_a.astype(jnp.bfloat16), x, y)

    with jax.named_scope("normalize"):
        normed = lax.optimization_barrier(normalize(tokens_in[0]))
        target_heads = heads_of(targets[0])
        target_a = jnp.concatenate([rolled(target_heads, 0), rolled(target_heads, 1)], axis=1)
        target_b = jnp.concatenate([rolled(target_heads, 2), rolled(target_heads, 3)], axis=1)
    key_scale = 1.0 / math.sqrt(width)
    grad_scale = 1.0 / math.sqrt(total_tokens)

    def partial_grad(field, target):
        keys = jnp.dot(normed, field, preferred_element_type=jnp.float32)
        residual = (keys * key_scale - target.astype(jnp.float32)).astype(jnp.bfloat16)
        grad = lax.dot_general(
            normed, residual, (((0,), (0,)), ((), ())), preferred_element_type=jnp.float32
        )
        return grad * grad_scale

    with jax.named_scope("products_a"):
        partial_a = partial_grad(field_a, target_a)
    with jax.named_scope("products_b"):
        partial_b = partial_grad(field_b, target_b)
    with jax.named_scope("scatter_a"):
        grad_a = scatter_a(partial_a, x, y)
    with jax.named_scope("scatter_b"):
        grad_b = scatter_b(partial_b, z)
    size = grad_a.shape[1] // 2
    grad_heads = [grad_a[:, :size], grad_a[:, size:], grad_b[:, :size], grad_b[:, size:]]
    grad = jnp.concatenate(
        [pick(grad_heads, (i + HEADS - 1 - fragment) % HEADS) for i in range(HEADS)], axis=1
    )
    with jax.named_scope("adam"):
        stepped, mean_next, var_next = adam_update(start_field, grad, adam_mean[0], adam_var[0])
        stepped_piece = pick(heads_of(stepped), fragment)
        mixed = blend_share * anchor_next + (1.0 - blend_share) * stepped_piece
        finished = replace_head(stepped, jnp.where(flag == 1, mixed, stepped_piece), fragment)
    return (finished[None], mean_next[None], var_next[None], new_anchor, new_momentum)


def solution(mesh):
    in_specs = (
        P("replica", "fsdp", None),
        P("replica", "fsdp", None),
        P("replica", "fsdp", None),
        P("replica", "fsdp", None),
        P("replica", "fsdp", None),
        P("fsdp", None),
        P("fsdp", None),
        P("replica", "fsdp", None),
        P(),
        P("replica"),
    )
    out_specs = (
        P("replica", "fsdp", None),
        P("replica", "fsdp", None),
        P("replica", "fsdp", None),
        P("fsdp", None),
        P("fsdp", None),
    )
    return jax.shard_map(
        on_device, mesh=mesh, in_specs=in_specs, out_specs=out_specs, check_vma=False
    )
```

```python
import math

import jax
import jax.numpy as jnp
from jax import lax
from jax.sharding import PartitionSpec as P

beta_first = 0.9
beta_second = 0.95
adam_epsilon = 1e-08
adam_steps = 20.0
inner_rate = 0.1
weight_decay = 0.1
outer_rate = 0.7
outer_pull = 0.9
blend_share = 0.5
norm_epsilon = 1e-05

NX, NY, NZ = 4, 2, 8
NXY = NX * NY
HEADS = 4


def fsdp_index(x, y, z):
    return (x % NX * NY + y % NY) * NZ + z % NZ


def shift(dx, dy, dz):
    return [
        (fsdp_index(x, y, z), fsdp_index(x + dx, y + dy, z + dz))
        for x in range(NX)
        for y in range(NY)
        for z in range(NZ)
    ]


X_UP, X_DOWN, Y_SWAP = shift(1, 0, 0), shift(-1, 0, 0), shift(0, 1, 0)
Z_UP, Z_DOWN = shift(0, 0, 1), shift(0, 0, -1)
Z_GROUPS = [[xy * NZ + z for z in range(NZ)] for xy in range(NXY)]
XY_GROUPS = [[xy * NZ + z for xy in range(NXY)] for z in range(NZ)]


def send(values, pairs):
    return lax.ppermute(values, "fsdp", pairs)


def exchange(values, groups):
    return lax.all_to_all(values, "fsdp", 0, 0, axis_index_groups=groups, tiled=True)


def normalize(rows):
    wide = rows.astype(jnp.float32)
    stat = jnp.mean(wide * wide, axis=-1, keepdims=True)
    return (wide * lax.rsqrt(stat + norm_epsilon)).astype(jnp.bfloat16)


def adam_update(start_field, grad, first, second):
    mean_next = beta_first * first + (1.0 - beta_first) * grad
    var_next = beta_second * second + (1.0 - beta_second) * grad * grad
    first_fix = 1.0 - beta_first**adam_steps
    second_fix = 1.0 - beta_second**adam_steps
    ratio = mean_next / first_fix / (jnp.sqrt(var_next / second_fix) + adam_epsilon)
    return (start_field - inner_rate * (ratio + weight_decay * start_field), mean_next, var_next)


def heads_of(field):
    size = field.shape[-1] // HEADS
    return [field[..., i * size : (i + 1) * size] for i in range(HEADS)]


def pick(choices, which):
    out = choices[0]
    for i in range(1, HEADS):
        out = jnp.where(which == i, choices[i], out)
    return out


def replace_head(field, piece, fragment):
    return jnp.concatenate(
        [jnp.where(fragment == i, piece, head) for i, head in enumerate(heads_of(field))], axis=-1
    )


def pack(total, terms):
    return (total * (0.5 / terms)).astype(jnp.float16)


def unpack(message, terms):
    return message.astype(jnp.float32) * (2.0 * terms)


class Chain:
    def __init__(self, steps):
        self.steps = steps
        self.values = None

    def go(self, times=1):
        for _ in range(times):
            self.values = self.steps.send(self.values)
        return self.values


def together(*chains):
    flat, tree = jax.tree.flatten([chain.values for chain in chains])
    values = jax.tree.unflatten(tree, lax.optimization_barrier(flat))
    for chain, value in zip(chains, values):
        chain.values = value


def thirds(rows):
    step = rows // 3 // 16 * 16
    return step, 2 * step


def block_of(x, y):
    return (x + NX) % NX * NY + (y + NY) % NY


def gather_xy(own, x, y):
    rows, cols = own.shape
    low, high, side = yield send(own, X_UP), send(own, X_DOWN), send(own, Y_SWAP)
    far, low_side, high_side = yield send(high, X_DOWN), send(side, X_UP), send(high, Y_SWAP)
    a, b = thirds(rows)
    far_side = yield (
        send(high_side[:a], X_DOWN),
        send(low_side[a:b], X_UP),
        send(far[b:], Y_SWAP),
    )
    whole = jnp.zeros((NXY, rows, cols), own.dtype)
    for dx, dy, piece in (
        (0, 0, own),
        (-1, 0, low),
        (1, 0, high),
        (0, 1, side),
        (2, 0, far),
        (-1, 1, low_side),
        (1, 1, high_side),
    ):
        whole = lax.dynamic_update_slice(whole, piece[None], (block_of(x + dx, y + dy), 0, 0))
    for start, piece in zip((0, a, b), far_side):
        whole = lax.dynamic_update_slice(whole, piece[None], (block_of(x + 2, y + 1), start, 0))
    return whole


def scatter_xy(blocks, x, y, terms):
    _, rows, cols = blocks.shape

    def mine(dx, dy, start=0, stop=rows):
        return lax.dynamic_slice(
            blocks, (block_of(x + dx, y + dy), start, 0), (1, stop - start, cols)
        )[0]

    a, b = thirds(rows)
    one, two, eight = terms, 2 * terms, 8 * terms
    to_high_side, to_low_side, to_far = yield (
        send(pack(mine(2, 1, 0, a), one), X_UP),
        send(pack(mine(2, 1, a, b), one), X_DOWN),
        send(pack(mine(2, 1, b, rows), one), Y_SWAP),
    )
    far = mine(2, 0) + jnp.pad(unpack(to_far, one), ((b, 0), (0, 0)))
    low_side = mine(-1, 1) + jnp.pad(unpack(to_low_side, one), ((a, rows - b), (0, 0)))
    high_side = mine(1, 1) + jnp.pad(unpack(to_high_side, one), ((0, rows - a), (0, 0)))
    from_far, from_low_side, from_high_side = yield (
        send(pack(far, two), X_UP),
        send(pack(low_side, two), X_DOWN),
        send(pack(high_side, two), Y_SWAP),
    )
    high = mine(1, 0) + unpack(from_far, two) + unpack(from_high_side, two)
    side = mine(0, 1) + unpack(from_low_side, two)
    high, low, side = yield (
        send(pack(high, eight), X_UP),
        send(pack(mine(-1, 0), eight), X_DOWN),
        send(pack(side, eight), Y_SWAP),
    )
    return mine(0, 0) + unpack(high, eight) + unpack(low, eight) + unpack(side, eight)


def gather_a(shard, x, y):
    rows, cols = shard.shape
    own = yield exchange(jnp.broadcast_to(shard, (NZ, rows, cols)), Z_GROUPS)
    whole = yield from gather_xy(own.reshape(NZ * rows, cols), x, y)
    yield whole.reshape(NXY * NZ * rows, cols)


def gather_b(shard, z):
    rows, cols = shard.shape
    own = yield exchange(jnp.broadcast_to(shard, (NXY, rows, cols)), XY_GROUPS)
    own = own.reshape(NXY, rows, cols)
    half = NXY // 2
    ups, downs = [own], [own]
    for step in range(1, NZ // 2):
        up, down = yield send(ups[-1], Z_UP), send(downs[-1], Z_DOWN)
        ups.append(up)
        downs.append(down)
    up, down = yield send(ups[-1][:half], Z_UP), send(downs[-1][half:], Z_DOWN)
    whole = jnp.zeros((NXY, NZ, rows, cols), shard.dtype)
    whole = lax.dynamic_update_slice(whole, own[:, None], (0, z, 0, 0))
    for step in range(1, NZ // 2):
        whole = lax.dynamic_update_slice(whole, ups[step][:, None], (0, (z - step) % NZ, 0, 0))
        whole = lax.dynamic_update_slice(whole, downs[step][:, None], (0, (z + step) % NZ, 0, 0))
    whole = lax.dynamic_update_slice(whole, up[:, None], (0, (z + NZ // 2) % NZ, 0, 0))
    whole = lax.dynamic_update_slice(whole, down[:, None], (half, (z + NZ // 2) % NZ, 0, 0))
    yield whole.reshape(NXY * NZ * rows, cols)


def scatter_a(partial, x, y):
    rows, cols = partial.shape[0] // (NXY * NZ), partial.shape[1]
    total = yield from scatter_xy(partial.reshape(NXY, NZ * rows, cols), x, y, 1)
    message = exchange(pack(total, 8).reshape(NZ, rows, cols), Z_GROUPS)
    yield jnp.sum(unpack(message.reshape(NZ, rows, cols), 8), axis=0)


def scatter_b(partial, z):
    rows, cols = partial.shape[0] // (NXY * NZ), partial.shape[1]
    blocks = partial.reshape(NXY, NZ, rows, cols)
    half = NXY // 2

    def mine(dz, start=0, stop=NXY):
        return lax.dynamic_slice(
            blocks, (start, (z + dz + NZ) % NZ, 0, 0), (stop - start, 1, rows, cols)
        )[:, 0]

    up, down = yield (
        send(pack(mine(4, 0, half), 4), Z_UP),
        send(pack(mine(-4, half, NXY), 4), Z_DOWN),
    )
    up = mine(3) + jnp.pad(unpack(up, 4), ((0, half), (0, 0), (0, 0)))
    down = mine(-3) + jnp.pad(unpack(down, 4), ((half, 0), (0, 0), (0, 0)))
    for step in (2, 1, 0):
        up, down = yield send(pack(up, 4), Z_UP), send(pack(down, 4), Z_DOWN)
        up, down = unpack(up, 4), unpack(down, 4)
        if step:
            up, down = mine(step) + up, mine(-step) + down
    message = exchange(pack(mine(0) + up + down, 8), XY_GROUPS)
    yield jnp.sum(unpack(message.reshape(NXY, rows, cols), 8), axis=0)


def on_device(
    tokens_in,
    targets,
    weights,
    adam_mean,
    adam_var,
    anchor,
    outer_momentum,
    pseudo_grad,
    fragment,
    delay,
):
    width = tokens_in.shape[2]
    total_tokens = tokens_in.shape[1] * lax.axis_size("fsdp")
    flag = delay[0]
    position = lax.axis_index("fsdp")
    x, y, z = position // (NY * NZ), position // NZ % NY, position % NZ

    with jax.named_scope("outer_update"):
        own = pseudo_grad[0]
        pair, cross, cross_pair = (
            lax.ppermute(own, "replica", [(i, i ^ k) for i in range(lax.axis_size("replica"))])
            for k in (1, 2, 3)
        )
        average = ((own + pair) + (cross + cross_pair)) / lax.axis_size("replica")
        moment_next = outer_pull * pick(heads_of(outer_momentum), fragment) + average
        anchor_next = pick(heads_of(anchor), fragment) - outer_rate * (
            average + outer_pull * moment_next
        )
        new_anchor = replace_head(anchor, anchor_next, fragment)
        new_momentum = replace_head(outer_momentum, moment_next, fragment)

    local = weights[0]
    local_heads = heads_of(local)
    local_piece = pick(local_heads, fragment)
    merged = blend_share * anchor_next + (1.0 - blend_share) * local_piece
    start_piece = jnp.where(flag == 0, merged, local_piece)
    start_field = replace_head(local, start_piece, fragment)

    def rolled(heads, k):
        return pick(heads, (fragment + 1 + k) % HEADS)

    shard_a = jnp.concatenate([rolled(local_heads, 2), start_piece], axis=1).astype(jnp.bfloat16)
    shard_b = jnp.concatenate([rolled(local_heads, 0), rolled(local_heads, 1)], axis=1)
    shard_b = shard_b.astype(jnp.bfloat16)
    with jax.named_scope("normalize"):
        normed = lax.optimization_barrier(normalize(tokens_in[0]))
        target_heads = heads_of(targets[0])
    key_scale = 1.0 / math.sqrt(width)
    grad_scale = 1.0 / math.sqrt(total_tokens)

    def partial_grad(field, target):
        keys = jnp.dot(normed, field, preferred_element_type=jnp.float32)
        residual = (keys * key_scale - target.astype(jnp.float32)).astype(jnp.bfloat16)
        grad = lax.dot_general(
            normed,
            lax.optimization_barrier(residual),
            (((0,), (0,)), ((), ())),
            preferred_element_type=jnp.float32,
        )
        return grad * grad_scale

    with jax.named_scope("gather"):
        b = Chain(gather_b(shard_b, z))
        b.values, shard_a = lax.optimization_barrier((b.go(), shard_a))
        a = Chain(gather_a(shard_a, x, y))
        for _ in range(4):
            a.go()
            together(a)
            b.go()
            together(b)
        field_a, field_b = a.go(), b.go()
    with jax.named_scope("products_a"):
        target = jnp.concatenate([rolled(target_heads, 2), rolled(target_heads, 3)], axis=1)
        partial_a = partial_grad(field_a, target)
    with jax.named_scope("products_b"):
        target = jnp.concatenate([rolled(target_heads, 0), rolled(target_heads, 1)], axis=1)
        partial_b = partial_grad(field_b, target)
    with jax.named_scope("scatter"):
        a = Chain(scatter_a(partial_a, x, y))
        b = Chain(scatter_b(partial_b, z))
        for _ in range(3):
            a.go()
            together(a)
        for _ in range(4):
            b.go()
            together(b)
        grad_a, grad_b = a.go(), b.go()
    grad_heads = heads_of(jnp.concatenate([grad_b, grad_a], axis=1))
    grad = jnp.concatenate(
        [pick(grad_heads, (i + HEADS - 1 - fragment) % HEADS) for i in range(HEADS)], axis=1
    )
    with jax.named_scope("adam"):
        stepped, mean_next, var_next = adam_update(start_field, grad, adam_mean[0], adam_var[0])
        stepped_piece = pick(heads_of(stepped), fragment)
        mixed = blend_share * anchor_next + (1.0 - blend_share) * stepped_piece
        finished = replace_head(stepped, jnp.where(flag == 1, mixed, stepped_piece), fragment)
    return (finished[None], mean_next[None], var_next[None], new_anchor, new_momentum)


def solution(mesh):
    in_specs = (
        P("replica", "fsdp", None),
        P("replica", "fsdp", None),
        P("replica", "fsdp", None),
        P("replica", "fsdp", None),
        P("replica", "fsdp", None),
        P("fsdp", None),
        P("fsdp", None),
        P("replica", "fsdp", None),
        P(),
        P("replica"),
    )
    out_specs = (
        P("replica", "fsdp", None),
        P("replica", "fsdp", None),
        P("replica", "fsdp", None),
        P("fsdp", None),
        P("fsdp", None),
    )
    return jax.shard_map(
        on_device, mesh=mesh, in_specs=in_specs, out_specs=out_specs, check_vma=False
    )
```

```python
import math

import jax
import jax.numpy as jnp
from jax import lax
from jax.experimental import pallas as pl
from jax.experimental.pallas import tpu as pltpu
from jax.sharding import PartitionSpec as P

beta_first = 0.9
beta_second = 0.95
adam_epsilon = 1e-08
adam_steps = 20.0
inner_rate = 0.1
weight_decay = 0.1
outer_rate = 0.7
outer_pull = 0.9
blend_share = 0.5
norm_epsilon = 1e-05

NX, NY, NZ = 4, 2, 8
NXY = NX * NY
HEADS = 4


def fsdp_index(x, y, z):
    return (x % NX * NY + y % NY) * NZ + z % NZ


def shift(dx, dy, dz):
    return [
        (fsdp_index(x, y, z), fsdp_index(x + dx, y + dy, z + dz))
        for x in range(NX)
        for y in range(NY)
        for z in range(NZ)
    ]


X_UP, X_DOWN, Y_SWAP = shift(1, 0, 0), shift(-1, 0, 0), shift(0, 1, 0)
Z_UP, Z_DOWN = shift(0, 0, 1), shift(0, 0, -1)
Z_GROUPS = [[xy * NZ + z for z in range(NZ)] for xy in range(NXY)]
XY_GROUPS = [[xy * NZ + z for xy in range(NXY)] for z in range(NZ)]


def send(values, pairs):
    return lax.ppermute(values, "fsdp", pairs)


def exchange(values, groups):
    return lax.all_to_all(values, "fsdp", 0, 0, axis_index_groups=groups, tiled=True)


def row_scale(rows):
    wide = rows.astype(jnp.float32)
    stat = jnp.mean(wide * wide, axis=-1, keepdims=True)
    return lax.rsqrt(stat + norm_epsilon)


def normalize_kernel(order_ref, scale_ref, whole_ref, *refs):
    *pieces, out_a_ref, out_b_ref = refs
    scale = scale_ref[...]
    out_a_ref[...] = (whole_ref[...].astype(jnp.float32) * scale).astype(jnp.bfloat16)
    cols = out_b_ref.shape[1] // len(pieces)
    for i, piece in enumerate(pieces):
        rows = piece[...].astype(jnp.float32) * scale
        out_b_ref[:, i * cols : (i + 1) * cols] = rows.astype(jnp.bfloat16)


def normalize(tokens, scale, order):
    rows, width = tokens.shape
    blocks = order.shape[1]
    wide = width // blocks
    narrow = wide // blocks

    def place(k):
        return pl.BlockSpec((rows, narrow), lambda i, order: (0, order[1, i] + k * blocks))

    return pl.pallas_call(
        normalize_kernel,
        grid_spec=pltpu.PrefetchScalarGridSpec(
            num_scalar_prefetch=1,
            grid=(blocks,),
            in_specs=[
                pl.BlockSpec((rows, 1), lambda i, order: (0, 0)),
                pl.BlockSpec((rows, wide), lambda i, order: (0, order[0, i])),
            ]
            + [place(k) for k in range(blocks)],
            out_specs=[pl.BlockSpec((rows, wide), lambda i, order: (0, i))] * 2,
        ),
        out_shape=[jax.ShapeDtypeStruct((rows, width), jnp.bfloat16)] * 2,
        compiler_params=pltpu.CompilerParams(vmem_limit_bytes=56 * 2**20),
        cost_estimate=pl.CostEstimate(
            flops=4 * rows * width, bytes_accessed=8 * rows * width, transcendentals=0
        ),
    )(order, scale, *[tokens] * (blocks + 1))


def adam_update(start_field, grad, first, second):
    mean_next = beta_first * first + (1.0 - beta_first) * grad
    var_next = beta_second * second + (1.0 - beta_second) * grad * grad
    first_fix = 1.0 - beta_first**adam_steps
    second_fix = 1.0 - beta_second**adam_steps
    ratio = mean_next / first_fix / (jnp.sqrt(var_next / second_fix) + adam_epsilon)
    return (start_field - inner_rate * (ratio + weight_decay * start_field), mean_next, var_next)


def heads_of(field):
    size = field.shape[-1] // HEADS
    return [field[..., i * size : (i + 1) * size] for i in range(HEADS)]


def pick(choices, which):
    out = choices[0]
    for i in range(1, HEADS):
        out = jnp.where(which == i, choices[i], out)
    return out


def replace_head(field, piece, fragment):
    return jnp.concatenate(
        [jnp.where(fragment == i, piece, head) for i, head in enumerate(heads_of(field))], axis=-1
    )


def pack(total, terms):
    return (total * (0.5 / terms)).astype(jnp.float16)


def unpack(message, terms):
    return message.astype(jnp.float32) * (2.0 * terms)


class Chain:
    def __init__(self, steps):
        self.steps = steps
        self.brought = []

    def go(self, *others):
        values = None
        if self.brought:
            values, _ = lax.optimization_barrier((self.brought[-1], others))
        self.brought.append(self.steps.send(values))
        return self.brought[-1]


XY_ORDER = ((0, 0), (-1, 0), (1, 0), (0, 1), (2, 0), (-1, 1), (1, 1), (2, 1))
Z_ORDER = (0, -1, 1, -2, 2, -3, 3, 4)
PART = 128


def thirds(rows):
    step = -(-rows // (3 * PART)) * PART
    return step, rows - step


def gather_a(shard):
    rows, cols = shard.shape
    copies = jnp.broadcast_to(shard, (NZ, rows, cols)).reshape(NZ * rows, cols)
    own = yield exchange(copies, Z_GROUPS)
    low, high, side = yield send(own, X_UP), send(own, X_DOWN), send(own, Y_SWAP)
    far, low_side, high_side = yield send(high, X_DOWN), send(side, X_UP), send(high, Y_SWAP)
    a, b = thirds(NZ * rows)
    far_side = yield (
        send(high_side[:a], X_DOWN),
        send(low_side[a:b], X_UP),
        send(far[b:], Y_SWAP),
    )
    yield [own, low, high, side, far, low_side, high_side, *far_side]


def gather_b(shard):
    rows, cols = shard.shape
    copies = jnp.broadcast_to(shard, (NXY, rows, cols)).reshape(NXY * rows, cols)
    own = yield exchange(copies, XY_GROUPS)
    half = NXY * rows // 2
    up, down = own, own
    pieces = [own]
    for _ in range(1, NZ // 2):
        up, down = yield send(up, Z_UP), send(down, Z_DOWN)
        pieces += [up, down]
    up, down = yield send(up[:half], Z_UP), send(down[half:], Z_DOWN)
    yield [*pieces, up, down]


def scatter_a(partial):
    rows = partial.shape[0] // NXY
    a, b = thirds(rows)

    def mine(dx, dy, start=0, stop=rows):
        first = XY_ORDER.index((dx, dy)) * rows
        return partial[first + start : first + stop]

    to_high_side, to_low_side, to_far = yield (
        send(pack(mine(2, 1, 0, a), 1), X_UP),
        send(pack(mine(2, 1, a, b), 1), X_DOWN),
        send(pack(mine(2, 1, b, rows), 1), Y_SWAP),
    )
    far = mine(2, 0) + jnp.pad(unpack(to_far, 1), ((b, 0), (0, 0)))
    low_side = mine(-1, 1) + jnp.pad(unpack(to_low_side, 1), ((a, rows - b), (0, 0)))
    high_side = mine(1, 1) + jnp.pad(unpack(to_high_side, 1), ((0, rows - a), (0, 0)))
    from_far, from_low_side, from_high_side = yield (
        send(pack(far, 2), X_UP),
        send(pack(low_side, 2), X_DOWN),
        send(pack(high_side, 2), Y_SWAP),
    )
    high = mine(1, 0) + unpack(from_far, 2) + unpack(from_high_side, 2)
    high, low, side = yield (
        send(pack(high, 8), X_UP),
        send(pack(mine(-1, 0), 8), X_DOWN),
        send(pack(mine(0, 1) + unpack(from_low_side, 2), 8), Y_SWAP),
    )
    total = mine(0, 0) + unpack(high, 8) + unpack(low, 8) + unpack(side, 8)
    message = exchange(pack(total, 8), Z_GROUPS)
    yield jnp.sum(unpack(message, 8).reshape(NZ, rows // NZ, -1), axis=0)


def scatter_b(partial):
    rows = partial.shape[0] // NZ
    half = rows // 2

    def mine(dz, start=0, stop=rows):
        first = Z_ORDER.index(dz) * rows
        return partial[first + start : first + stop]

    up, down = yield send(pack(mine(4, 0, half), 4), Z_UP), send(pack(mine(4, half), 4), Z_DOWN)
    up = mine(3) + jnp.pad(unpack(up, 4), ((0, half), (0, 0)))
    down = mine(-3) + jnp.pad(unpack(down, 4), ((half, 0), (0, 0)))
    for step in (2, 1, 0):
        up, down = yield send(pack(up, 4), Z_UP), send(pack(down, 4), Z_DOWN)
        up, down = unpack(up, 4), unpack(down, 4)
        if step:
            up, down = mine(step) + up, mine(-step) + down
    message = exchange(pack(mine(0) + up + down, 8), XY_GROUPS)
    yield jnp.sum(unpack(message, 8).reshape(NXY, rows // NXY, -1), axis=0)


def on_device(
    tokens_in,
    targets,
    weights,
    adam_mean,
    adam_var,
    anchor,
    outer_momentum,
    pseudo_grad,
    fragment,
    delay,
):
    width = tokens_in.shape[2]
    total_tokens = tokens_in.shape[1] * lax.axis_size("fsdp")
    flag = delay[0]
    position = lax.axis_index("fsdp")
    x, y, z = position // (NY * NZ), position // NZ % NY, position % NZ

    with jax.named_scope("outer_update"):
        own = pseudo_grad[0]
        pair, cross, cross_pair = (
            lax.ppermute(own, "replica", [(i, i ^ k) for i in range(lax.axis_size("replica"))])
            for k in (1, 2, 3)
        )
        average = ((own + pair) + (cross + cross_pair)) / lax.axis_size("replica")
        moment_next = outer_pull * pick(heads_of(outer_momentum), fragment) + average
        anchor_next = pick(heads_of(anchor), fragment) - outer_rate * (
            average + outer_pull * moment_next
        )
        new_anchor = replace_head(anchor, anchor_next, fragment)
        new_momentum = replace_head(outer_momentum, moment_next, fragment)

    local = weights[0]
    local_heads = heads_of(local)
    local_piece = pick(local_heads, fragment)
    merged = blend_share * anchor_next + (1.0 - blend_share) * local_piece
    start_piece = jnp.where(flag == 0, merged, local_piece)
    start_field = replace_head(local, start_piece, fragment)

    def rolled(heads, k):
        return pick(heads, (fragment + 1 + k) % HEADS)

    shard_a = jnp.concatenate([rolled(local_heads, 2), start_piece], axis=1).astype(jnp.bfloat16)
    shard_b = jnp.concatenate([rolled(local_heads, 0), rolled(local_heads, 1)], axis=1)
    shard_b = shard_b.astype(jnp.bfloat16)
    with jax.named_scope("normalize"):
        tokens = tokens_in[0]
        scale = row_scale(tokens)
        order_a = [(x + dx + NX) % NX * NY + (y + dy) % NY for dx, dy in XY_ORDER]
        order_b = [(z + dz + NZ) % NZ for dz in Z_ORDER]
        target_heads = heads_of(targets[0])
    key_scale = 1.0 / math.sqrt(width)
    grad_scale = 1.0 / math.sqrt(total_tokens)

    def partial_grad(normed, pieces, target):
        keys, start = 0.0, 0
        for piece in pieces:
            stop = start + piece.shape[0]
            keys += jnp.dot(normed[:, start:stop], piece, preferred_element_type=jnp.float32)
            start = stop
        residual = (keys * key_scale - target.astype(jnp.float32)).astype(jnp.bfloat16)
        grad = lax.dot_general(
            normed,
            lax.optimization_barrier(residual),
            (((0,), (0,)), ((), ())),
            preferred_element_type=jnp.float32,
        )
        return grad * grad_scale

    with jax.named_scope("gather"):
        b = Chain(gather_b(shard_b))
        _, shard_a = lax.optimization_barrier((b.go(), shard_a))
        _, scale = lax.optimization_barrier((b.brought[0], scale))
        order = jnp.stack([jnp.stack(order_a), jnp.stack(order_b)]).astype(jnp.int32)
        normed_a, normed_b = normalize(tokens, scale, order)
        a = Chain(gather_a(shard_a))
        a.go()
        b.go()
        b.go()
        a.go(b.brought[1])
        b.go(a.brought[0])
        a.go(b.brought[2])
        b.go(a.brought[1])
        a.go(b.brought[3])
        field_b = b.go(a.brought[2])
        field_a = a.go(b.brought[4])
        gathered = a.brought[3]
    with jax.named_scope("products_b"):
        target = jnp.concatenate([rolled(target_heads, 0), rolled(target_heads, 1)], axis=1)
        partial_b = partial_grad(normed_b, field_b, target)
    with jax.named_scope("products_a"):
        target = jnp.concatenate([rolled(target_heads, 2), rolled(target_heads, 3)], axis=1)
        partial_a = partial_grad(normed_a, field_a, target)
    with jax.named_scope("scatter"):
        a = Chain(scatter_a(partial_a))
        b = Chain(scatter_b(partial_b))
        b.go()
        a.go()
        b.go(gathered)
        a.go(b.brought[0])
        b.go(a.brought[0])
        a.go(b.brought[1])
        b.go(a.brought[1])
        grad_a = a.go(b.brought[2])
        grad_b = b.go(grad_a)
        grad_b, new_anchor, new_momentum = lax.optimization_barrier(
            (grad_b, new_anchor, new_momentum)
        )
    grad_heads = heads_of(jnp.concatenate([grad_b, grad_a], axis=1))
    grad = jnp.concatenate(
        [pick(grad_heads, (i + HEADS - 1 - fragment) % HEADS) for i in range(HEADS)], axis=1
    )
    with jax.named_scope("adam"):
        stepped, mean_next, var_next = adam_update(start_field, grad, adam_mean[0], adam_var[0])
        stepped_piece = pick(heads_of(stepped), fragment)
        mixed = blend_share * anchor_next + (1.0 - blend_share) * stepped_piece
        finished = replace_head(stepped, jnp.where(flag == 1, mixed, stepped_piece), fragment)
    return (finished[None], mean_next[None], var_next[None], new_anchor, new_momentum)


def solution(mesh):
    in_specs = (
        P("replica", "fsdp", None),
        P("replica", "fsdp", None),
        P("replica", "fsdp", None),
        P("replica", "fsdp", None),
        P("replica", "fsdp", None),
        P("fsdp", None),
        P("fsdp", None),
        P("replica", "fsdp", None),
        P(),
        P("replica"),
    )
    out_specs = (
        P("replica", "fsdp", None),
        P("replica", "fsdp", None),
        P("replica", "fsdp", None),
        P("fsdp", None),
        P("fsdp", None),
    )
    return jax.shard_map(
        on_device, mesh=mesh, in_specs=in_specs, out_specs=out_specs, check_vma=False
    )
```

```python
import math

import jax
import jax.numpy as jnp
from jax import lax
from jax.experimental import pallas as pl
from jax.experimental.pallas import tpu as pltpu
from jax.sharding import PartitionSpec as P

beta_first = 0.9
beta_second = 0.95
adam_epsilon = 1e-08
adam_steps = 20.0
inner_rate = 0.1
weight_decay = 0.1
outer_rate = 0.7
outer_pull = 0.9
blend_share = 0.5
norm_epsilon = 1e-05

NX, NY, NZ = 4, 2, 8
NXY = NX * NY
HEADS = 4


def fsdp_index(x, y, z):
    return (x % NX * NY + y % NY) * NZ + z % NZ


def shift(dx, dy, dz):
    return [
        (fsdp_index(x, y, z), fsdp_index(x + dx, y + dy, z + dz))
        for x in range(NX)
        for y in range(NY)
        for z in range(NZ)
    ]


X_UP, X_DOWN, Y_SWAP = shift(1, 0, 0), shift(-1, 0, 0), shift(0, 1, 0)
Z_UP, Z_DOWN = shift(0, 0, 1), shift(0, 0, -1)
Z_GROUPS = [[xy * NZ + z for z in range(NZ)] for xy in range(NXY)]
XY_GROUPS = [[xy * NZ + z for xy in range(NXY)] for z in range(NZ)]


def send(values, pairs):
    return lax.ppermute(values, "fsdp", pairs)


def exchange(values, groups):
    return lax.all_to_all(values, "fsdp", 0, 0, axis_index_groups=groups, tiled=True)


def row_scale(rows):
    wide = rows.astype(jnp.float32)
    stat = jnp.mean(wide * wide, axis=-1, keepdims=True)
    return lax.rsqrt(stat + norm_epsilon)


def normalize_kernel(order_ref, scale_ref, whole_ref, *refs):
    *pieces, out_a_ref, out_b_ref = refs
    scale = scale_ref[...]
    out_a_ref[...] = (whole_ref[...].astype(jnp.float32) * scale).astype(jnp.bfloat16)
    cols = out_b_ref.shape[1] // len(pieces)
    for i, piece in enumerate(pieces):
        rows = piece[...].astype(jnp.float32) * scale
        out_b_ref[:, i * cols : (i + 1) * cols] = rows.astype(jnp.bfloat16)


def normalize(tokens, scale, order):
    rows, width = tokens.shape
    blocks = order.shape[1]
    wide = width // blocks
    narrow = wide // blocks

    def place(k):
        return pl.BlockSpec((rows, narrow), lambda i, order: (0, order[1, i] + k * blocks))

    return pl.pallas_call(
        normalize_kernel,
        grid_spec=pltpu.PrefetchScalarGridSpec(
            num_scalar_prefetch=1,
            grid=(blocks,),
            in_specs=[
                pl.BlockSpec((rows, 1), lambda i, order: (0, 0)),
                pl.BlockSpec((rows, wide), lambda i, order: (0, order[0, i])),
            ]
            + [place(k) for k in range(blocks)],
            out_specs=[pl.BlockSpec((rows, wide), lambda i, order: (0, i))] * 2,
        ),
        out_shape=[jax.ShapeDtypeStruct((rows, width), jnp.bfloat16)] * 2,
        compiler_params=pltpu.CompilerParams(vmem_limit_bytes=56 * 2**20),
        cost_estimate=pl.CostEstimate(
            flops=4 * rows * width, bytes_accessed=8 * rows * width, transcendentals=0
        ),
    )(order, scale, *[tokens] * (blocks + 1))


def adam_update(start_field, grad, first, second):
    mean_next = beta_first * first + (1.0 - beta_first) * grad
    var_next = beta_second * second + (1.0 - beta_second) * grad * grad
    first_fix = 1.0 - beta_first**adam_steps
    second_fix = 1.0 - beta_second**adam_steps
    ratio = mean_next / first_fix / (jnp.sqrt(var_next / second_fix) + adam_epsilon)
    return (start_field - inner_rate * (ratio + weight_decay * start_field), mean_next, var_next)


def heads_of(field):
    size = field.shape[-1] // HEADS
    return [field[..., i * size : (i + 1) * size] for i in range(HEADS)]


def pick(choices, which):
    out = choices[0]
    for i in range(1, HEADS):
        out = jnp.where(which == i, choices[i], out)
    return out


def replace_head(field, piece, fragment):
    return jnp.concatenate(
        [jnp.where(fragment == i, piece, head) for i, head in enumerate(heads_of(field))], axis=-1
    )


def pack(total, terms):
    return (total * (0.5 / terms)).astype(jnp.float16)


def unpack(message, terms):
    return message.astype(jnp.float32) * (2.0 * terms)


class Chain:
    def __init__(self, steps):
        self.steps = steps
        self.brought = []

    def go(self, *others):
        values = None
        if self.brought:
            values, _ = lax.optimization_barrier((self.brought[-1], others))
        self.brought.append(self.steps.send(values))
        return self.brought[-1]


XY_ORDER = ((0, 0), (-1, 0), (1, 0), (0, 1), (2, 0), (-1, 1), (1, 1), (2, 1))
Z_ORDER = (0, -1, 1, -2, 2, -3, 3, 4)
PART = 128


def thirds(rows):
    step = -(-rows // (3 * PART)) * PART
    return step, rows - step


def gather_a(shard):
    rows, cols = shard.shape
    copies = jnp.broadcast_to(shard, (NZ, rows, cols)).reshape(NZ * rows, cols)
    own = yield exchange(copies, Z_GROUPS)
    low, high, side = yield send(own, X_UP), send(own, X_DOWN), send(own, Y_SWAP)
    far, low_side, high_side = yield send(high, X_DOWN), send(side, X_UP), send(high, Y_SWAP)
    a, b = thirds(NZ * rows)
    far_side = yield (
        send(high_side[:a], X_DOWN),
        send(low_side[a:b], X_UP),
        send(far[b:], Y_SWAP),
    )
    yield [own, low, high, side, far, low_side, high_side, *far_side]


def gather_b(copies):
    own = yield exchange(copies, XY_GROUPS)
    half = copies.shape[0] // 2
    up, down = own, own
    pieces = [own]
    for _ in range(1, NZ // 2):
        up, down = yield send(up, Z_UP), send(down, Z_DOWN)
        pieces += [up, down]
    up, down = yield send(up[:half], Z_UP), send(down[half:], Z_DOWN)
    yield [*pieces, up, down]


def scatter_a(partial):
    rows = partial.shape[0] // NXY
    a, b = thirds(rows)

    def mine(dx, dy, start=0, stop=rows):
        first = XY_ORDER.index((dx, dy)) * rows
        return partial[first + start : first + stop]

    to_high_side, to_low_side, to_far = yield (
        send(pack(mine(2, 1, 0, a), 1), X_UP),
        send(pack(mine(2, 1, a, b), 1), X_DOWN),
        send(pack(mine(2, 1, b, rows), 1), Y_SWAP),
    )
    far = mine(2, 0) + jnp.pad(unpack(to_far, 1), ((b, 0), (0, 0)))
    low_side = mine(-1, 1) + jnp.pad(unpack(to_low_side, 1), ((a, rows - b), (0, 0)))
    high_side = mine(1, 1) + jnp.pad(unpack(to_high_side, 1), ((0, rows - a), (0, 0)))
    from_far, from_low_side, from_high_side = yield (
        send(pack(far, 2), X_UP),
        send(pack(low_side, 2), X_DOWN),
        send(pack(high_side, 2), Y_SWAP),
    )
    high = mine(1, 0) + unpack(from_far, 2) + unpack(from_high_side, 2)
    high, low, side = yield (
        send(pack(high, 8), X_UP),
        send(pack(mine(-1, 0), 8), X_DOWN),
        send(pack(mine(0, 1) + unpack(from_low_side, 2), 8), Y_SWAP),
    )
    total = mine(0, 0) + unpack(high, 8) + unpack(low, 8) + unpack(side, 8)
    message = exchange(pack(total, 8), Z_GROUPS)
    yield jnp.sum(unpack(message, 8).reshape(NZ, rows // NZ, -1), axis=0)


def scatter_b(partial):
    rows = partial.shape[0] // NZ
    half = rows // 2

    def mine(dz, start=0, stop=rows):
        first = Z_ORDER.index(dz) * rows
        return partial[first + start : first + stop]

    up, down = yield send(pack(mine(4, 0, half), 4), Z_UP), send(pack(mine(4, half), 4), Z_DOWN)
    up = mine(3) + jnp.pad(unpack(up, 4), ((0, half), (0, 0)))
    down = mine(-3) + jnp.pad(unpack(down, 4), ((half, 0), (0, 0)))
    for step in (2, 1, 0):
        up, down = yield send(pack(up, 4), Z_UP), send(pack(down, 4), Z_DOWN)
        up, down = unpack(up, 4), unpack(down, 4)
        if step:
            up, down = mine(step) + up, mine(-step) + down
    message = exchange(pack(mine(0) + up + down, 8), XY_GROUPS)
    yield jnp.sum(unpack(message, 8).reshape(NXY, rows // NXY, -1), axis=0)


def on_device(
    tokens_in,
    targets,
    weights,
    adam_mean,
    adam_var,
    anchor,
    outer_momentum,
    pseudo_grad,
    fragment,
    delay,
):
    width = tokens_in.shape[2]
    total_tokens = tokens_in.shape[1] * lax.axis_size("fsdp")
    flag = delay[0]
    position = lax.axis_index("fsdp")
    x, y, z = position // (NY * NZ), position // NZ % NY, position % NZ

    def rolled(heads, k):
        return pick(heads, (fragment + 1 + k) % HEADS)

    local = weights[0]
    first = heads_of(local)
    shard_b = jnp.concatenate([rolled(first, 0), rolled(first, 1)], axis=1).astype(jnp.bfloat16)
    copies_b = jnp.broadcast_to(shard_b, (NXY, *shard_b.shape)).reshape(-1, shard_b.shape[1])
    copies_b, own, local = lax.optimization_barrier((copies_b, pseudo_grad[0], local))

    with jax.named_scope("outer_update"):
        pair, cross, cross_pair = (
            lax.ppermute(own, "replica", [(i, i ^ k) for i in range(lax.axis_size("replica"))])
            for k in (1, 2, 3)
        )
        average = ((own + pair) + (cross + cross_pair)) / lax.axis_size("replica")
        moment_next = outer_pull * pick(heads_of(outer_momentum), fragment) + average
        anchor_next = pick(heads_of(anchor), fragment) - outer_rate * (
            average + outer_pull * moment_next
        )
        new_anchor = replace_head(anchor, anchor_next, fragment)
        new_momentum = replace_head(outer_momentum, moment_next, fragment)

    local_heads = heads_of(local)
    local_piece = pick(local_heads, fragment)
    merged = blend_share * anchor_next + (1.0 - blend_share) * local_piece
    start_piece = jnp.where(flag == 0, merged, local_piece)
    start_field = replace_head(local, start_piece, fragment)

    shard_a = jnp.concatenate([rolled(local_heads, 2), start_piece], axis=1).astype(jnp.bfloat16)
    with jax.named_scope("normalize"):
        tokens = tokens_in[0]
        scale = row_scale(tokens)
        order_a = [(x + dx + NX) % NX * NY + (y + dy) % NY for dx, dy in XY_ORDER]
        order_b = [(z + dz + NZ) % NZ for dz in Z_ORDER]
        target_heads = heads_of(targets[0])
    key_scale = 1.0 / math.sqrt(width)
    grad_scale = 1.0 / math.sqrt(total_tokens)

    def partial_grad(normed, pieces, target):
        keys, start = 0.0, 0
        for piece in pieces:
            stop = start + piece.shape[0]
            keys += jnp.dot(normed[:, start:stop], piece, preferred_element_type=jnp.float32)
            start = stop
        residual = (keys * key_scale - target.astype(jnp.float32)).astype(jnp.bfloat16)
        grad = lax.dot_general(
            normed,
            lax.optimization_barrier(residual),
            (((0,), (0,)), ((), ())),
            preferred_element_type=jnp.float32,
        )
        return grad * grad_scale

    with jax.named_scope("gather"):
        b = Chain(gather_b(copies_b))
        _, shard_a = lax.optimization_barrier((b.go(), shard_a))
        _, scale = lax.optimization_barrier((b.brought[0], scale))
        order = jnp.stack([jnp.stack(order_a), jnp.stack(order_b)]).astype(jnp.int32)
        normed_a, normed_b = normalize(tokens, scale, order)
        a = Chain(gather_a(shard_a))
        a.go()
        b.go()
        b.go()
        a.go(b.brought[1])
        b.go(a.brought[0])
        a.go(b.brought[2])
        b.go(a.brought[1])
        a.go(b.brought[3])
        field_b = b.go(a.brought[2])
        field_a = a.go(b.brought[4])
        gathered = a.brought[3]
    with jax.named_scope("products_b"):
        target = jnp.concatenate([rolled(target_heads, 0), rolled(target_heads, 1)], axis=1)
        partial_b = partial_grad(normed_b, field_b, target)
    with jax.named_scope("products_a"):
        target = jnp.concatenate([rolled(target_heads, 2), rolled(target_heads, 3)], axis=1)
        partial_a = partial_grad(normed_a, field_a, target)
    with jax.named_scope("scatter"):
        a = Chain(scatter_a(partial_a))
        b = Chain(scatter_b(partial_b))
        b.go()
        a.go()
        b.go(gathered)
        a.go(b.brought[0])
        b.go(a.brought[0])
        a.go(b.brought[1])
        b.go(a.brought[1])
        grad_a = a.go(b.brought[2])
        grad_b = b.go(grad_a)
        grad_b, new_anchor, new_momentum = lax.optimization_barrier(
            (grad_b, new_anchor, new_momentum)
        )
    grad_heads = heads_of(jnp.concatenate([grad_b, grad_a], axis=1))
    grad = jnp.concatenate(
        [pick(grad_heads, (i + HEADS - 1 - fragment) % HEADS) for i in range(HEADS)], axis=1
    )
    with jax.named_scope("adam"):
        stepped, mean_next, var_next = adam_update(start_field, grad, adam_mean[0], adam_var[0])
        stepped_piece = pick(heads_of(stepped), fragment)
        mixed = blend_share * anchor_next + (1.0 - blend_share) * stepped_piece
        finished = replace_head(stepped, jnp.where(flag == 1, mixed, stepped_piece), fragment)
    return (finished[None], mean_next[None], var_next[None], new_anchor, new_momentum)


def solution(mesh):
    in_specs = (
        P("replica", "fsdp", None),
        P("replica", "fsdp", None),
        P("replica", "fsdp", None),
        P("replica", "fsdp", None),
        P("replica", "fsdp", None),
        P("fsdp", None),
        P("fsdp", None),
        P("replica", "fsdp", None),
        P(),
        P("replica"),
    )
    out_specs = (
        P("replica", "fsdp", None),
        P("replica", "fsdp", None),
        P("replica", "fsdp", None),
        P("fsdp", None),
        P("fsdp", None),
    )
    return jax.shard_map(
        on_device, mesh=mesh, in_specs=in_specs, out_specs=out_specs, check_vma=False
    )
```

```python
import math

import jax
import jax.numpy as jnp
from jax import lax
from jax.experimental import pallas as pl
from jax.experimental.pallas import tpu as pltpu
from jax.sharding import PartitionSpec as P

beta_first = 0.9
beta_second = 0.95
adam_epsilon = 1e-08
adam_steps = 20.0
inner_rate = 0.1
weight_decay = 0.1
outer_rate = 0.7
outer_pull = 0.9
blend_share = 0.5
norm_epsilon = 1e-05

NX, NY, NZ = 4, 2, 8
NXY = NX * NY
HEADS = 4


def fsdp_index(x, y, z):
    return (x % NX * NY + y % NY) * NZ + z % NZ


def shift(dx, dy, dz):
    return [
        (fsdp_index(x, y, z), fsdp_index(x + dx, y + dy, z + dz))
        for x in range(NX)
        for y in range(NY)
        for z in range(NZ)
    ]


X_UP, X_DOWN, Y_SWAP = shift(1, 0, 0), shift(-1, 0, 0), shift(0, 1, 0)
Z_UP, Z_DOWN = shift(0, 0, 1), shift(0, 0, -1)
Z_GROUPS = [[xy * NZ + z for z in range(NZ)] for xy in range(NXY)]
XY_GROUPS = [[xy * NZ + z for xy in range(NXY)] for z in range(NZ)]


def send(values, pairs):
    return lax.ppermute(values, "fsdp", pairs)


def exchange(values, groups):
    return lax.all_to_all(values, "fsdp", 0, 0, axis_index_groups=groups, tiled=True)


def row_scale(rows):
    wide = rows.astype(jnp.float32)
    stat = jnp.mean(wide * wide, axis=-1, keepdims=True)
    return lax.rsqrt(stat + norm_epsilon)


def normalize_kernel(order_ref, scale_ref, whole_ref, *refs):
    *pieces, out_a_ref, out_b_ref = refs
    scale = scale_ref[...]
    out_a_ref[...] = (whole_ref[...].astype(jnp.float32) * scale).astype(jnp.bfloat16)
    cols = out_b_ref.shape[1] // len(pieces)
    for i, piece in enumerate(pieces):
        rows = piece[...].astype(jnp.float32) * scale
        out_b_ref[:, i * cols : (i + 1) * cols] = rows.astype(jnp.bfloat16)


def normalize(tokens, scale, order):
    rows, width = tokens.shape
    blocks = order.shape[1]
    wide = width // blocks
    narrow = wide // blocks

    def place(k):
        return pl.BlockSpec((rows, narrow), lambda i, order: (0, order[1, i] + k * blocks))

    return pl.pallas_call(
        normalize_kernel,
        grid_spec=pltpu.PrefetchScalarGridSpec(
            num_scalar_prefetch=1,
            grid=(blocks,),
            in_specs=[
                pl.BlockSpec((rows, 1), lambda i, order: (0, 0)),
                pl.BlockSpec((rows, wide), lambda i, order: (0, order[0, i])),
            ]
            + [place(k) for k in range(blocks)],
            out_specs=[pl.BlockSpec((rows, wide), lambda i, order: (0, i))] * 2,
        ),
        out_shape=[jax.ShapeDtypeStruct((rows, width), jnp.bfloat16)] * 2,
        compiler_params=pltpu.CompilerParams(vmem_limit_bytes=56 * 2**20),
        cost_estimate=pl.CostEstimate(
            flops=4 * rows * width, bytes_accessed=8 * rows * width, transcendentals=0
        ),
    )(order, scale, *[tokens] * (blocks + 1))


def adam_update(start_field, grad, first, second):
    mean_next = beta_first * first + (1.0 - beta_first) * grad
    var_next = beta_second * second + (1.0 - beta_second) * grad * grad
    first_fix = 1.0 - beta_first**adam_steps
    second_fix = 1.0 - beta_second**adam_steps
    ratio = mean_next / first_fix / (jnp.sqrt(var_next / second_fix) + adam_epsilon)
    return (start_field - inner_rate * (ratio + weight_decay * start_field), mean_next, var_next)


def heads_of(field):
    size = field.shape[-1] // HEADS
    return [field[..., i * size : (i + 1) * size] for i in range(HEADS)]


def pick(choices, which):
    out = choices[0]
    for i in range(1, HEADS):
        out = jnp.where(which == i, choices[i], out)
    return out


def replace_head(field, piece, fragment):
    return jnp.concatenate(
        [jnp.where(fragment == i, piece, head) for i, head in enumerate(heads_of(field))], axis=-1
    )


def pack(total, terms):
    return (total * (0.5 / terms)).astype(jnp.float16)


def unpack(message, terms):
    return message.astype(jnp.float32) * (2.0 * terms)


class Chain:
    def __init__(self, steps):
        self.steps = steps
        self.brought = []

    def go(self, *others):
        values = None
        if self.brought:
            values, _ = lax.optimization_barrier((self.brought[-1], others))
        self.brought.append(self.steps.send(values))
        return self.brought[-1]


XY_ORDER = ((0, 0), (-1, 0), (1, 0), (0, 1), (2, 0), (-1, 1), (1, 1), (2, 1))
Z_ORDER = (0, -1, 1, -2, 2, -3, 3, 4)
PART = 128


def thirds(rows):
    step = -(-rows // (3 * PART)) * PART
    return step, rows - step


def gather_a(shard):
    rows, cols = shard.shape
    copies = jnp.broadcast_to(shard, (NZ, rows, cols)).reshape(NZ * rows, cols)
    own = yield exchange(copies, Z_GROUPS)
    low, high, side = yield send(own, X_UP), send(own, X_DOWN), send(own, Y_SWAP)
    far, low_side, high_side = yield send(high, X_DOWN), send(side, X_UP), send(high, Y_SWAP)
    a, b = thirds(NZ * rows)
    far_side = yield (
        send(high_side[:a], X_DOWN),
        send(low_side[a:b], X_UP),
        send(far[b:], Y_SWAP),
    )
    yield [own, low, high, side, far, low_side, high_side, *far_side]


def gather_b(copies):
    own = yield exchange(copies, XY_GROUPS)
    half = copies.shape[0] // 2
    up, down = own, own
    pieces = [own]
    for _ in range(1, NZ // 2):
        up, down = yield send(up, Z_UP), send(down, Z_DOWN)
        pieces += [up, down]
    up, down = yield send(up[:half], Z_UP), send(down[half:], Z_DOWN)
    yield [*pieces, up, down]


def scatter_a(partial):
    rows = partial.shape[0] // NXY
    a, b = thirds(rows)

    def mine(dx, dy, start=0, stop=rows):
        first = XY_ORDER.index((dx, dy)) * rows
        return partial[first + start : first + stop]

    to_high_side, to_low_side, to_far = yield (
        send(pack(mine(2, 1, 0, a), 1), X_UP),
        send(pack(mine(2, 1, a, b), 1), X_DOWN),
        send(pack(mine(2, 1, b, rows), 1), Y_SWAP),
    )
    far = mine(2, 0) + jnp.pad(unpack(to_far, 1), ((b, 0), (0, 0)))
    low_side = mine(-1, 1) + jnp.pad(unpack(to_low_side, 1), ((a, rows - b), (0, 0)))
    high_side = mine(1, 1) + jnp.pad(unpack(to_high_side, 1), ((0, rows - a), (0, 0)))
    from_far, from_low_side, from_high_side = yield (
        send(pack(far, 2), X_UP),
        send(pack(low_side, 2), X_DOWN),
        send(pack(high_side, 2), Y_SWAP),
    )
    high = mine(1, 0) + unpack(from_far, 2) + unpack(from_high_side, 2)
    high, low, side = yield (
        send(pack(high, 8), X_UP),
        send(pack(mine(-1, 0), 8), X_DOWN),
        send(pack(mine(0, 1) + unpack(from_low_side, 2), 8), Y_SWAP),
    )
    total = mine(0, 0) + unpack(high, 8) + unpack(low, 8) + unpack(side, 8)
    message = exchange(pack(total, 8), Z_GROUPS)
    yield jnp.sum(unpack(message, 8).reshape(NZ, rows // NZ, -1), axis=0)


def scatter_b(partial, packed):
    rows = partial.shape[0] // NZ
    half = rows // 2

    def mine(dz, start=0, stop=rows):
        first = Z_ORDER.index(dz) * rows
        return partial[first + start : first + stop]

    up, down = yield send(pack(mine(4, 0, half), 4), Z_UP), send(pack(mine(4, half), 4), Z_DOWN)
    up = mine(3) + jnp.pad(unpack(up, 4), ((0, half), (0, 0)))
    down = mine(-3) + jnp.pad(unpack(down, 4), ((half, 0), (0, 0)))
    for step in (2, 1, 0):
        packed.append((pack(up, 4), pack(down, 4)))
        up, down = yield send(packed[-1][0], Z_UP), send(packed[-1][1], Z_DOWN)
        up, down = unpack(up, 4), unpack(down, 4)
        if step:
            up, down = mine(step) + up, mine(-step) + down
    message = exchange(pack(mine(0) + up + down, 8), XY_GROUPS)
    yield jnp.sum(unpack(message, 8).reshape(NXY, rows // NXY, -1), axis=0)


def on_device(
    tokens_in,
    targets,
    weights,
    adam_mean,
    adam_var,
    anchor,
    outer_momentum,
    pseudo_grad,
    fragment,
    delay,
):
    width = tokens_in.shape[2]
    total_tokens = tokens_in.shape[1] * lax.axis_size("fsdp")
    flag = delay[0]
    position = lax.axis_index("fsdp")
    x, y, z = position // (NY * NZ), position // NZ % NY, position % NZ

    def rolled(heads, k):
        return pick(heads, (fragment + 1 + k) % HEADS)

    local = weights[0]
    first = heads_of(local)
    shard_b = jnp.concatenate([rolled(first, 0), rolled(first, 1)], axis=1).astype(jnp.bfloat16)
    copies_b = jnp.broadcast_to(shard_b, (NXY, *shard_b.shape)).reshape(-1, shard_b.shape[1])
    copies_b, own, local = lax.optimization_barrier((copies_b, pseudo_grad[0], local))

    with jax.named_scope("outer_update"):
        pair, cross, cross_pair = (
            lax.ppermute(own, "replica", [(i, i ^ k) for i in range(lax.axis_size("replica"))])
            for k in (1, 2, 3)
        )
        average = ((own + pair) + (cross + cross_pair)) / lax.axis_size("replica")
        moment_next = outer_pull * pick(heads_of(outer_momentum), fragment) + average
        anchor_next = pick(heads_of(anchor), fragment) - outer_rate * (
            average + outer_pull * moment_next
        )
        new_anchor = replace_head(anchor, anchor_next, fragment)
        new_momentum = replace_head(outer_momentum, moment_next, fragment)

    local_heads = heads_of(local)
    local_piece = pick(local_heads, fragment)
    merged = blend_share * anchor_next + (1.0 - blend_share) * local_piece
    start_piece = jnp.where(flag == 0, merged, local_piece)
    start_field = replace_head(local, start_piece, fragment)

    shard_a = jnp.concatenate([rolled(local_heads, 2), start_piece], axis=1).astype(jnp.bfloat16)
    with jax.named_scope("normalize"):
        tokens = tokens_in[0]
        scale = row_scale(tokens)
        order_a = [(x + dx + NX) % NX * NY + (y + dy) % NY for dx, dy in XY_ORDER]
        order_b = [(z + dz + NZ) % NZ for dz in Z_ORDER]
        target_heads = heads_of(targets[0])
    key_scale = 1.0 / math.sqrt(width)
    grad_scale = 1.0 / math.sqrt(total_tokens)

    def partial_grad(normed, pieces, target):
        keys, start = 0.0, 0
        for piece in pieces:
            stop = start + piece.shape[0]
            keys += jnp.dot(normed[:, start:stop], piece, preferred_element_type=jnp.float32)
            start = stop
        residual = (keys * key_scale - target.astype(jnp.float32)).astype(jnp.bfloat16)
        grad = lax.dot_general(
            normed,
            lax.optimization_barrier(residual),
            (((0,), (0,)), ((), ())),
            preferred_element_type=jnp.float32,
        )
        return grad * grad_scale

    with jax.named_scope("gather"):
        b = Chain(gather_b(copies_b))
        _, shard_a = lax.optimization_barrier((b.go(), shard_a))
        _, scale = lax.optimization_barrier((b.brought[0], scale))
        order = jnp.stack([jnp.stack(order_a), jnp.stack(order_b)]).astype(jnp.int32)
        normed_a, normed_b = normalize(tokens, scale, order)
        a = Chain(gather_a(shard_a))
        a.go()
        b.go()
        b.go()
        a.go(b.brought[1])
        b.go(a.brought[0])
        a.go(b.brought[2])
        b.go(a.brought[1])
        a.go(b.brought[3])
        field_b = b.go(a.brought[2])
        field_a = a.go(b.brought[4])
        gathered = a.brought[3]
    with jax.named_scope("products_b"):
        target = jnp.concatenate([rolled(target_heads, 0), rolled(target_heads, 1)], axis=1)
        partial_b = partial_grad(normed_b, field_b, target)
    with jax.named_scope("products_a"):
        target = jnp.concatenate([rolled(target_heads, 2), rolled(target_heads, 3)], axis=1)
        partial_a = partial_grad(normed_a, field_a, target)
    with jax.named_scope("scatter"):
        a = Chain(scatter_a(partial_a))
        packed = []
        b = Chain(scatter_b(partial_b, packed))
        b.go()
        a.go()
        b.go(gathered)
        a.go(b.brought[0])
        b.go(a.brought[0])
        a.go(b.brought[1])
        b.go(a.brought[1])
        grad_a = a.go(packed[-1])
        grad_b = b.go(grad_a)
        grad_b, new_anchor, new_momentum = lax.optimization_barrier(
            (grad_b, new_anchor, new_momentum)
        )
    grad_heads = heads_of(jnp.concatenate([grad_b, grad_a], axis=1))
    grad = jnp.concatenate(
        [pick(grad_heads, (i + HEADS - 1 - fragment) % HEADS) for i in range(HEADS)], axis=1
    )
    with jax.named_scope("adam"):
        stepped, mean_next, var_next = adam_update(start_field, grad, adam_mean[0], adam_var[0])
        stepped_piece = pick(heads_of(stepped), fragment)
        mixed = blend_share * anchor_next + (1.0 - blend_share) * stepped_piece
        finished = replace_head(stepped, jnp.where(flag == 1, mixed, stepped_piece), fragment)
    return (finished[None], mean_next[None], var_next[None], new_anchor, new_momentum)


def solution(mesh):
    in_specs = (
        P("replica", "fsdp", None),
        P("replica", "fsdp", None),
        P("replica", "fsdp", None),
        P("replica", "fsdp", None),
        P("replica", "fsdp", None),
        P("fsdp", None),
        P("fsdp", None),
        P("replica", "fsdp", None),
        P(),
        P("replica"),
    )
    out_specs = (
        P("replica", "fsdp", None),
        P("replica", "fsdp", None),
        P("replica", "fsdp", None),
        P("fsdp", None),
        P("fsdp", None),
    )
    return jax.shard_map(
        on_device, mesh=mesh, in_specs=in_specs, out_specs=out_specs, check_vma=False
    )
```
